32 devices in a mesh: parts: 1, train: 32 (over z, y, x, core).
Axes of the slice: x: 2, y: 2, z: 4, core: 2. Of those that a mesh axis runs over, the one named last changes fastest.
Arguments:
- train_layer_input: bfloat16 [16384, 4096], P(('parts', 'train')), may hold values from -6 to 6
- train_output_gradient: bfloat16 [16384, 4096], P(('parts', 'train')), may hold values from -6 to 6
- train_example_index: int32 [32, 512], P(('parts', 'train')), may hold values from 0 to 31, never falling along the last dimension, each value on 1 to 32 neighbouring positions
- eval_layer_input: bfloat16 [4096, 4096], P(('parts', 'train')), may hold values from -6 to 6
- eval_output_gradient: bfloat16 [4096, 4096], P(('parts', 'train')), may hold values from -6 to 6
- eval_rollout_index: int32 [32, 128], P(('parts', 'train')), may hold values from 0 to 15, never falling along the last dimension, each value on 1 to 16 neighbouring positions
- adapter_down: bfloat16 [4096, 16], replicated, may hold values from -0.09375 to 0.09375
- adapter_up: bfloat16 [16, 4096], replicated, may hold values from -0.09375 to 0.09375
- gradient_projector: bfloat16 [4096, 256], P('train'), may hold values from -0.09375 to 0.09375
- input_projector: bfloat16 [4096, 256], P('train'), may hold values from -0.09375 to 0.09375
- paired_eval_index: int32 [32, 16], P('parts'), may hold values from 0 to 31, all different within a row
- live_slot_count: int32 [32], P('parts'), may hold values from 1 to 16, as said below
Outputs:
- scores: float32 [32, 16, 32, 16], P(('parts', 'train'))
The draws below stay inside these ranges and needn't reach their ends.
Inputs may be any that keep to these rules, and one draw needn't show every extreme that they name: Each train block's slots name distinct eval blocks; slots from live_slot_count onward are unused; some train block uses all 16 slots.
All inputs are finite; a program needn't handle non-finite values.
Results may differ from the reference program's by a relative error of at most 0.004.
Values may be sent and summed in bfloat16 or wider, within the bound.
No kernel may reach another device: no remote copies, remote signals or barrier semaphores. Data moves between devices by JAX's collectives and lax.ppermute only.
A program may use at most 128 MiB of HBM per device.

```python
import math
import jax
import jax.numpy as jnp
import numpy as np
from jax import lax

MODEL_WIDTH = 4096
ADAPTER_RANK = 16
PW = 256
K = 8192
TOK_T = 512
TOK_E = 128
TRAIN_EXAMPLES = 32
EVAL_ROLLOUTS = 16
SLOTS = 16
SEG_T = 32
SEG_E = 16
TBLOCKS = 32


def draw_live_slot_count(key, part):
    key = jax.random.fold_in(key, 7)
    first_key, second_key = jax.random.split(key)
    counts = jax.random.randint(first_key, (TBLOCKS,), 1, SLOTS + 1)
    fullest = jax.random.randint(second_key, (), 0, TBLOCKS)
    return jnp.where(jnp.arange(TBLOCKS) == fullest, SLOTS, counts).astype(jnp.int32)


def block_scale(stream_key, extent, cuts, least, top_value):
    factor_of = 1.0
    for dim, blocks in cuts:
        steps = jax.random.uniform(jax.random.fold_in(jax.random.fold_in(stream_key, 6), dim), (blocks,), jnp.float32, least / len(cuts), top_value / len(cuts))
        factor_of = factor_of * jnp.repeat(jnp.exp(steps), extent[dim] // blocks).reshape((-1,) + (1,) * (len(extent) - 1 - dim))
    return factor_of


def distinct(own_key, rows, number_of, top, lift):
    ranking = jax.random.permutation(jax.random.fold_in(own_key, 1), number_of)
    pull = ranking
    for power in range(3):
        pull = pull * pull // number_of
    pull = pull * lift // number_of
    chance = jax.random.randint(jax.random.fold_in(own_key, 2), (rows, number_of), 0, 4096) + pull
    holders = jax.random.permutation(jax.random.fold_in(own_key, 3), rows)[jnp.arange(number_of) % rows]
    chance = jnp.where(jnp.arange(rows)[:, None] == holders[None, :], 1 << 14, chance)
    priority = chance * number_of + jnp.arange(number_of)
    return lax.top_k(priority.astype(jnp.int32), top)[1].astype(jnp.int32)


def profile(amount, total, reach, lean):
    weights = [(1 << 20) // math.isqrt(rank ** lean) + 1 for rank in range(2, amount + 1)]
    rest, given = total - reach - (amount - 1), [1] * (amount - 1)
    while rest > 0:
        free = [i for i in range(amount - 1) if given[i] < reach]
        whole, budget = sum([weights[i] for i in free]), rest
        for i in free:
            more = min(reach - given[i], max(1, budget * weights[i] // whole), rest)
            given[i] = given[i] + more
            rest = rest - more
    return np.array([reach] + given)


def uneven(rng, count, total, bound, skew):
    if count == 2:
        one = jax.random.randint(rng, (), max(1, total - bound), min(bound, total - 1) + 1)
        return jnp.stack([one, total - one])
    lengths = jnp.asarray(profile(count, total, bound, skew), jnp.int32)
    pairs = (count - 1) // 2
    giver, taker = lengths[1:1 + 2 * pairs:2], lengths[2:2 + 2 * pairs:2]
    slack = jnp.minimum(giver - 1, bound - taker)
    passed = jax.random.randint(jax.random.fold_in(rng, 1), (pairs,), 0, 1 << 20) % (slack + 1)
    lengths = lengths.at[1:1 + 2 * pairs:2].set(giver - passed).at[2:2 + 2 * pairs:2].set(taker + passed)
    return lengths[jax.random.permutation(jax.random.fold_in(rng, 2), count)]


def gaussian(stream_key, shape, scale, most, cuts=(), kind=jnp.bfloat16):
    result = scale * jax.random.normal(stream_key, shape, jnp.float32)
    if cuts:
        result = result * block_scale(stream_key, shape, cuts, -0.22, 0.18)
    return jnp.clip(result, -most, most).astype(kind)


def setup_inputs(seed: int = 0, part: int = 0) -> dict:
    key_list = jax.random.split(jax.random.key(seed), 13)
    own_keys = jax.random.split(jax.random.fold_in(key_list[12], part), 13)
    train_layer_input = gaussian(own_keys[0], (TBLOCKS * TOK_T, MODEL_WIDTH), 1.0, 6.0, ((0, 32),))
    train_output_gradient = gaussian(own_keys[1], (TBLOCKS * TOK_T, MODEL_WIDTH), 1.0, 6.0, ((0, 32),))
    train_example_index = jax.vmap(lambda own: jnp.searchsorted(jnp.cumsum(uneven(own, TRAIN_EXAMPLES, TOK_T, SEG_T, 1)), jnp.arange(TOK_T), side="right"))(jax.random.split(own_keys[2], TBLOCKS)).reshape((TBLOCKS, TOK_T)).astype(jnp.int32)
    eval_layer_input = gaussian(own_keys[3], (TBLOCKS * TOK_E, MODEL_WIDTH), 1.0, 6.0, ((0, 32),))
    eval_output_gradient = gaussian(own_keys[4], (TBLOCKS * TOK_E, MODEL_WIDTH), 1.0, 6.0, ((0, 32),))
    eval_rollout_index = jax.vmap(lambda own: jnp.searchsorted(jnp.cumsum(uneven(own, EVAL_ROLLOUTS, TOK_E, SEG_E, 1)), jnp.arange(TOK_E), side="right"))(jax.random.split(own_keys[5], TBLOCKS)).reshape((TBLOCKS, TOK_E)).astype(jnp.int32)
    adapter_down = gaussian(key_list[6], (MODEL_WIDTH, ADAPTER_RANK), MODEL_WIDTH ** -0.5, 0.09375)
    adapter_up = gaussian(key_list[7], (ADAPTER_RANK, MODEL_WIDTH), MODEL_WIDTH ** -0.5, 0.09375)
    gradient_projector = gaussian(key_list[8], (MODEL_WIDTH, PW), MODEL_WIDTH ** -0.5, 0.09375, ((0, 32),))
    input_projector = gaussian(key_list[9], (MODEL_WIDTH, PW), MODEL_WIDTH ** -0.5, 0.09375, ((0, 32),))
    paired_eval_index = distinct(own_keys[10], TBLOCKS, TBLOCKS, SLOTS, 8192)
    live_slot_count = draw_live_slot_count(jax.random.fold_in(jax.random.fold_in(key_list[12], part), 71), part)
    return {"train_layer_input": train_layer_input, "train_output_gradient": train_output_gradient, "train_example_index": train_example_index, "eval_layer_input": eval_layer_input, "eval_output_gradient": eval_output_gradient, "eval_rollout_index": eval_rollout_index, "adapter_down": adapter_down, "adapter_up": adapter_up, "gradient_projector": gradient_projector, "input_projector": input_projector, "paired_eval_index": paired_eval_index, "live_slot_count": live_slot_count}


def example_features(hidden_down, backward_up, grad_proj, input_proj, segment_index, item_number):
    onehot = (segment_index[None, :] == jnp.arange(item_number, dtype=jnp.int32)[:, None]).astype(jnp.float32)
    weighted_a = onehot[:, :, None] * hidden_down[None, :, :]
    weighted_b = onehot[:, :, None] * backward_up[None, :, :]
    part_b = jnp.einsum('etr,tk->erk', weighted_a, grad_proj, precision=lax.Precision.HIGHEST)
    part_a = jnp.einsum('etr,tk->erk', weighted_b, input_proj, precision=lax.Precision.HIGHEST)
    raw = jnp.concatenate([part_b.reshape(item_number, -1), part_a.reshape(item_number, -1)], axis=1)
    raw = raw * lax.rsqrt(lax.optimization_barrier(jnp.mean(raw * raw, axis=1, keepdims=True)) + 1e-06)
    return raw.astype(jnp.bfloat16)

def block_feature_rows(input_list, gradient_list, segment_index, adapter_down, adapter_up, gradient_projector, input_projector, item_number):
    hidden_down = jnp.dot(input_list, adapter_down, preferred_element_type=jnp.float32)
    backward_up = jnp.dot(gradient_list, adapter_up.T, preferred_element_type=jnp.float32)
    grad_proj = jnp.dot(gradient_list, gradient_projector, preferred_element_type=jnp.float32)
    input_proj = jnp.dot(input_list, input_projector, preferred_element_type=jnp.float32)
    return example_features(hidden_down, backward_up, grad_proj, input_proj, segment_index, item_number)

def reference(train_layer_input, train_output_gradient, train_example_index, eval_layer_input, eval_output_gradient, eval_rollout_index, adapter_down, adapter_up, gradient_projector, input_projector, paired_eval_index, live_slot_count):

    def train_one(item_list):
        return block_feature_rows(item_list[0], item_list[1], item_list[2], adapter_down, adapter_up, gradient_projector, input_projector, TRAIN_EXAMPLES)

    def eval_one(item_list):
        return block_feature_rows(item_list[0], item_list[1], item_list[2], adapter_down, adapter_up, gradient_projector, input_projector, EVAL_ROLLOUTS)
    train_feats = lax.map(train_one, (train_layer_input.reshape(TBLOCKS, TOK_T, -1), train_output_gradient.reshape(TBLOCKS, TOK_T, -1), train_example_index))
    eval_feats = lax.map(eval_one, (eval_layer_input.reshape(TBLOCKS, TOK_E, -1), eval_output_gradient.reshape(TBLOCKS, TOK_E, -1), eval_rollout_index))
    factor = 1.0 / K ** 0.5

    def score_one(index):
        chosen = eval_feats[paired_eval_index[index]]
        tiles = jnp.einsum('ik,sjk->sij', train_feats[index], chosen, preferred_element_type=jnp.float32)
        live = (jnp.arange(SLOTS, dtype=jnp.int32) < live_slot_count[index]).astype(jnp.float32)
        return tiles * factor * live[:, None, None]
    return lax.map(score_one, jnp.arange(TBLOCKS, dtype=jnp.int32))
```

```python
import functools

import jax
import jax.numpy as jnp
from jax import lax
from jax.experimental import pallas as pl
from jax.experimental.pallas import tpu as pltpu
from jax.sharding import PartitionSpec as P

RANK = 16
PW = 256
K = 2 * RANK * PW
TRAIN_EXAMPLES = 32
EVAL_ROLLOUTS = 16
SLOTS = 16
EPS = 1e-06

VMEM = pl.BlockSpec(memory_space=pltpu.VMEM)
SMEM = pl.BlockSpec(memory_space=pltpu.SMEM)
ANY = pl.BlockSpec(memory_space=pl.ANY)
BF16 = jnp.bfloat16
F32 = jnp.float32
NT = (((1,), (1,)), ((), ()))
PARAMS = pltpu.CompilerParams(vmem_limit_bytes=56 * 1024 * 1024)


def xor_permute(block, mask, n):
    return lax.ppermute(block, "train", [(i, i ^ mask) for i in range(n)])


def gather_blocks(block, n):
    if n != 32:
        whole = lax.all_gather(block, "train", axis=0, tiled=True)
        return [(whole, list(range(n)))], False
    ways = [(0, (2, 4)), (8, (4, 2)), (16, (2, 4)), (24, (4, 2))]
    rows = [block] + [xor_permute(block, mask, n) for mask, _ in ways[1:]]
    pieces = []
    for own, (start, order) in zip(rows, ways):
        held, masks = own, [start]
        for mask in order:
            held = jnp.concatenate([held, xor_permute(held, mask, n)], axis=0)
            masks = masks + [m ^ mask for m in masks]
        pieces.append((held, masks))
    pieces += [(xor_permute(held, 1, n), [m ^ 1 for m in masks]) for held, masks in pieces]
    return pieces, True


def split(value):
    high = value.astype(BF16)
    return high, (value - high.astype(F32)).astype(BF16)


def dot3(left, right):
    lh, ll = split(left)
    rh, rl = split(right)
    dot = functools.partial(jnp.dot, preferred_element_type=F32)
    return dot(lh, rh) + (dot(lh, rl) + dot(ll, rh))


def one_hot(index_row, count):
    steps = lax.broadcasted_iota(jnp.int32, (count, index_row.shape[1]), 0)
    return (index_row == steps).astype(F32)


def weighted(rows, picked):
    ranks, tokens = rows.shape
    return (rows[:, None, :] * picked[None, :, :]).reshape(ranks * picked.shape[0], tokens)


def fetch(masks_of, refs, base, held, sem):
    copies = []
    for ref, masks in zip(refs, masks_of):
        for s, mask in enumerate(masks):
            copies.append(pltpu.make_async_copy(ref.at[s], held.at[base ^ mask], sem))
    for copy in copies:
        copy.start()
    pltpu.make_async_copy(held, held, sem).wait()


def squares(raw, items):
    each = jnp.sum(raw * raw, axis=1, keepdims=True)
    return jnp.sum(each.reshape(RANK, items, 1), axis=0)


def eval_kernel(masks_of, base_ref, x_ref, g_ref, hidden_ref, back_ref, index_ref, *rest):
    refs, (pack_ref, table_ref, held, sem) = rest[: len(masks_of)], rest[len(masks_of) :]
    fetch(masks_of, refs, base_ref[0], held, sem)
    count, height, _ = held.shape
    part = (height - 8) // 2
    width = count * part
    grad = jnp.dot(g_ref[...], held[:, 0:part, :].reshape(width, PW), preferred_element_type=F32)
    inp = jnp.dot(x_ref[...], held[:, part : 2 * part, :].reshape(width, PW), preferred_element_type=F32)
    picked = one_hot(index_ref[...], EVAL_ROLLOUTS)
    hidden, back = hidden_ref[...], back_ref[...]
    total = squares(dot3(weighted(hidden, picked), grad), EVAL_ROLLOUTS)
    total = total + squares(dot3(weighted(back, picked), inp), EVAL_ROLLOUTS)
    scale = lax.rsqrt(total * (1.0 / K) + EPS)
    per_token = jnp.sum(picked * scale, axis=0, keepdims=True)
    tokens = x_ref.shape[0]
    pack_ref[0, 0:tokens, :] = grad.astype(BF16)
    pack_ref[0, tokens : 2 * tokens, :] = inp.astype(BF16)
    pack_ref[0, 2 * tokens : 2 * tokens + RANK, 0:tokens] = (hidden * per_token).astype(BF16)
    pack_ref[0, 2 * tokens : 2 * tokens + RANK, tokens : 2 * tokens] = (back * per_token).astype(BF16)
    table_ref[...] = held[:, 2 * part : 2 * part + 8, 0:tokens].astype(F32)


def train_kernel(masks_of, base_ref, x_ref, g_ref, hidden_ref, back_ref, index_ref, *rest):
    refs, (feats_ref, held, sem) = rest[: len(masks_of)], rest[len(masks_of) :]
    fetch(masks_of, refs, base_ref[0], held, sem)
    count, height, _ = held.shape
    part = (height - 8) // 2
    width = count * part
    picked = one_hot(index_ref[...], TRAIN_EXAMPLES)
    grad = jnp.dot(g_ref[...], held[:, 0:part, :].reshape(width, PW), preferred_element_type=F32)
    raw_a = dot3(weighted(hidden_ref[...], picked), grad)
    inp = jnp.dot(x_ref[...], held[:, part : 2 * part, :].reshape(width, PW), preferred_element_type=F32)
    raw_b = dot3(weighted(back_ref[...], picked), inp)
    total = squares(raw_a, TRAIN_EXAMPLES) + squares(raw_b, TRAIN_EXAMPLES)
    scale = lax.rsqrt(total * (1.0 / K) + EPS)[None]
    shape = (RANK, TRAIN_EXAMPLES, PW)
    feats_ref[0] = (raw_a.reshape(shape) * scale).reshape(RANK * TRAIN_EXAMPLES, PW).astype(BF16)
    feats_ref[1] = (raw_b.reshape(shape) * scale).reshape(RANK * TRAIN_EXAMPLES, PW).astype(BF16)


def score_kernel(masks_of, base_ref, chosen_ref, live_ref, feats_ref, table_ref, *rest):
    refs, (out_ref, held, sem) = rest[: len(masks_of)], rest[len(masks_of) :]
    base = base_ref[0]
    for slot in range(SLOTS):
        mask = chosen_ref[slot] ^ base
        for ref, masks in zip(refs, masks_of):
            for s, own in enumerate(masks):

                @pl.when(mask == own)
                def _():
                    pltpu.make_async_copy(ref.at[s], held.at[slot], sem).start()

    pltpu.make_async_copy(held, held, sem).wait()
    tokens = (held.shape[1] - RANK) // 2
    shape = (RANK, TRAIN_EXAMPLES, 2 * tokens)
    dot = functools.partial(lax.dot_general, dimension_numbers=NT, preferred_element_type=F32)
    for pair in range(0, SLOTS, 2):
        two = slice(pair, pair + 2)
        grad = held[two, 0:tokens, :].reshape(2 * tokens, PW)
        inp = held[two, tokens : 2 * tokens, :].reshape(2 * tokens, PW)
        coef = held[two, 2 * tokens : 2 * tokens + RANK, :].astype(F32)
        hidden = jnp.concatenate([coef[0, :, 0:tokens], coef[1, :, 0:tokens]], axis=1)
        back = jnp.concatenate([coef[0, :, tokens:], coef[1, :, tokens:]], axis=1)
        mixed = jnp.sum(dot(feats_ref[0], grad).reshape(shape) * hidden[:, None, :], axis=0)
        mixed = mixed + jnp.sum(dot(feats_ref[1], inp).reshape(shape) * back[:, None, :], axis=0)
        high, low = split(mixed)
        for k in range(2):
            slot = pair + k
            index_row = table_ref[chosen_ref[slot], 0:1, :].astype(jnp.int32)
            picked = one_hot(index_row, EVAL_ROLLOUTS).astype(BF16)
            lanes = slice(k * tokens, (k + 1) * tokens)
            tile = dot(high[:, lanes], picked) + dot(low[:, lanes], picked)
            factor = jnp.where(slot < live_ref[0], 1.0 / K**0.5, 0.0)
            out_ref[0, slot] = tile * factor


def per_device(
    n,
    train_layer_input,
    train_output_gradient,
    train_example_index,
    eval_layer_input,
    eval_output_gradient,
    eval_rollout_index,
    adapter_down,
    adapter_up,
    gradient_projector,
    input_projector,
    paired_eval_index,
    live_slot_count,
):
    mine = lax.axis_index("train")
    tokens = eval_layer_input.shape[0]
    index_rows = jnp.pad(eval_rollout_index.astype(BF16), ((0, 7), (0, PW - tokens)))
    block = jnp.concatenate([gradient_projector, input_projector, index_rows], axis=0)[None]
    pieces, relative = gather_blocks(block, n)
    base = jnp.where(relative, mine, 0).astype(jnp.int32).reshape(1)
    arrays = [array for array, _ in pieces]
    masks_of = [masks for _, masks in pieces]

    def down(x):
        return lax.dot_general(adapter_down, x, (((0,), (1,)), ((), ())), preferred_element_type=F32)

    def up(g):
        return lax.dot_general(adapter_up, g, NT, preferred_element_type=F32)

    held = [pltpu.VMEM((n,) + block.shape[1:], BF16), pltpu.SemaphoreType.DMA]
    pack, table = pl.pallas_call(
        functools.partial(eval_kernel, masks_of),
        out_shape=[
            jax.ShapeDtypeStruct((1, 2 * tokens + RANK, PW), BF16),
            jax.ShapeDtypeStruct((n, 8, tokens), F32),
        ],
        in_specs=[SMEM] + [VMEM] * 5 + [ANY] * len(arrays),
        out_specs=[VMEM] * 2,
        scratch_shapes=held,
        compiler_params=PARAMS,
        cost_estimate=pl.CostEstimate(flops=10**9, bytes_accessed=7 * 2**20, transcendentals=0),
        name="eval_factors",
    )(
        base,
        eval_layer_input,
        eval_output_gradient,
        down(eval_layer_input),
        up(eval_output_gradient),
        eval_rollout_index,
        *arrays,
    )
    eval_pieces, _ = gather_blocks(pack, n)
    feats = pl.pallas_call(
        functools.partial(train_kernel, masks_of),
        out_shape=jax.ShapeDtypeStruct((2, RANK * TRAIN_EXAMPLES, PW), BF16),
        in_specs=[SMEM] + [VMEM] * 5 + [ANY] * len(arrays),
        out_specs=VMEM,
        scratch_shapes=held,
        compiler_params=PARAMS,
        cost_estimate=pl.CostEstimate(flops=4 * 10**9, bytes_accessed=12 * 2**20, transcendentals=0),
        name="train_features",
    )(
        base,
        train_layer_input,
        train_output_gradient,
        down(train_layer_input),
        up(train_output_gradient),
        train_example_index,
        *arrays,
    )
    chosen = lax.dynamic_index_in_dim(paired_eval_index, mine, 0, keepdims=False)
    live = lax.dynamic_index_in_dim(live_slot_count, mine, 0, keepdims=True)
    eval_arrays = [array for array, _ in eval_pieces]
    return pl.pallas_call(
        functools.partial(score_kernel, masks_of),
        out_shape=jax.ShapeDtypeStruct((1, SLOTS, TRAIN_EXAMPLES, EVAL_ROLLOUTS), F32),
        in_specs=[SMEM] * 3 + [VMEM] * 2 + [ANY] * len(eval_arrays),
        out_specs=VMEM,
        scratch_shapes=[pltpu.VMEM((SLOTS,) + pack.shape[1:], BF16), pltpu.SemaphoreType.DMA],
        compiler_params=PARAMS,
        cost_estimate=pl.CostEstimate(flops=2 * 10**9, bytes_accessed=3 * 2**20, transcendentals=0),
        name="score_tiles",
    )(base, chosen, live, feats, table, *eval_arrays)


def solution(mesh):
    in_specs = (
        P(("parts", "train"), None),
        P(("parts", "train"), None),
        P(("parts", "train"), None),
        P(("parts", "train"), None),
        P(("parts", "train"), None),
        P(("parts", "train"), None),
        P(),
        P(),
        P("train", None),
        P("train", None),
        P("parts", None),
        P("parts"),
    )
    out_specs = P(("parts", "train"), None, None, None)
    return jax.shard_map(
        functools.partial(per_device, mesh.shape["train"]),
        mesh=mesh,
        in_specs=in_specs,
        out_specs=out_specs,
        check_vma=False,
    )
```

```python
import functools

import jax
import jax.numpy as jnp
from jax import lax
from jax.experimental import pallas as pl
from jax.experimental.pallas import tpu as pltpu
from jax.sharding import PartitionSpec as P

RANK = 16
PW = 256
K = 2 * RANK * PW
TRAIN_EXAMPLES = 32
EVAL_ROLLOUTS = 16
SLOTS = 16
EPS = 1e-06

VMEM = pl.BlockSpec(memory_space=pltpu.VMEM)
SMEM = pl.BlockSpec(memory_space=pltpu.SMEM)
BF16 = jnp.bfloat16
F32 = jnp.float32
NT = (((1,), (1,)), ((), ()))


def gather_chunks(block, n, early, middle, late):
    if n != 32:
        whole = lax.all_gather(block, "train", axis=0, tiled=True)
        return None, [[(whole, list(range(n)))]], early, middle(early)

    def permute(held, mask):
        return lax.ppermute(held, "train", [(i, i ^ mask) for i in range(n)])

    orders = [(2, 4), (4, 2), (2, 4), (4, 2)]
    rows = [block] + [permute(block, mask) for mask in (8, 16, 24)]
    first, held, second, swapped = [permute(block, 2)], [], [], []
    first[0], rows[1], early = lax.optimization_barrier((first[0], rows[1], early))

    def join(chunk):
        held.append(jnp.concatenate([rows[chunk], first[chunk]], axis=0))

    def spread(chunk):
        second.append(permute(held[chunk], orders[chunk][1]))
        swapped.append(permute(held[chunk], 1))

    def finish(chunk):
        one, two = orders[chunk]
        return [
            (held[chunk], [0, one]),
            (second[chunk], [two, one ^ two]),
            (swapped[chunk], [1, one ^ 1]),
            (permute(second[chunk], 1), [two ^ 1, one ^ two ^ 1]),
        ]

    first.append(permute(rows[1], orders[1][0]))
    join(0)
    held[0], early = lax.optimization_barrier((held[0], early))
    spread(0)
    middle = middle(early)
    join(1)
    spread(1)
    rows[2], rows[3], middle = lax.optimization_barrier((rows[2], rows[3], middle))
    first.append(permute(rows[2], orders[2][0]))
    first.append(permute(rows[3], orders[3][0]))
    join(2)
    join(3)
    spread(2)
    spread(3)
    front = [finish(0), finish(1)]
    done = late(front, middle)
    second[2], second[3], done = lax.optimization_barrier((second[2], second[3], done))
    return (done, front), [finish(2), finish(3)], early, middle


def placed(n):
    mine = lax.axis_index("train").astype(jnp.int32)
    if n != 32:
        return jnp.zeros((2,), jnp.int32), n
    return jnp.stack([mine // 8, mine % 8]), 8


def plan(chunks, start):
    return (
        [(start + c, lows) for c, chunk in enumerate(chunks) for _, lows in chunk],
        [array for chunk in chunks for array, _ in chunk],
    )


def split(value):
    high = value.astype(BF16)
    return high, (value - high.astype(F32)).astype(BF16)


def dot3(left, right):
    lh, ll = split(left)
    rh, rl = split(right)
    dot = functools.partial(jnp.dot, preferred_element_type=F32)
    return dot(lh, rh) + (dot(lh, rl) + dot(ll, rh))


def one_hot(index_row, count):
    steps = lax.broadcasted_iota(jnp.int32, (count, index_row.shape[1]), 0)
    return (index_row == steps).astype(F32)


def weighted(rows, picked):
    ranks, tokens = rows.shape
    return (rows[:, None, :] * picked[None, :, :]).reshape(ranks * picked.shape[0], tokens)


def squares(raw, items):
    each = jnp.sum(raw * raw, axis=1, keepdims=True)
    return jnp.sum(each.reshape(RANK, items, 1), axis=0)


def project(steps, size, place_ref, x_ref, g_ref, refs, held, grad, inp):
    hi, lo = place_ref[0], place_ref[1]
    part = refs[0].shape[1] // 2
    start, width = steps[0][0], size * part
    for ref, (chunk, lows) in zip(refs, steps):
        for s, low in enumerate(lows):
            held[chunk - start, 0, lo ^ low] = ref[s, 0:part, :]
            held[chunk - start, 1, lo ^ low] = ref[s, part : 2 * part, :]
    for chunk in sorted({c for c, _ in steps}):
        columns = pl.ds(pl.multiple_of((hi ^ chunk) * width, width), width)
        more = jnp.dot(g_ref[:, columns], held[chunk - start, 0].reshape(width, PW), preferred_element_type=F32)
        grad = more if grad is None else grad + more
        more = jnp.dot(x_ref[:, columns], held[chunk - start, 1].reshape(width, PW), preferred_element_type=F32)
        inp = more if inp is None else inp + more
    return grad, inp


def begin_kernel(steps, size, place_ref, x_ref, g_ref, *rest):
    refs, (sums_ref, held) = rest[: len(steps)], rest[len(steps) :]
    grad, inp = project(steps, size, place_ref, x_ref, g_ref, refs, held, None, None)
    sums_ref[0] = grad
    sums_ref[1] = inp


def eval_kernel(steps, size, begun, place_ref, x_ref, g_ref, hidden_ref, back_ref, index_ref, *rest):
    refs, rest = rest[: len(steps)], rest[len(steps) :]
    pack_ref, held = rest[begun:]
    grad, inp = (rest[0][0], rest[0][1]) if begun else (None, None)
    grad, inp = project(steps, size, place_ref, x_ref, g_ref, refs, held, grad, inp)
    picked = one_hot(index_ref[...], EVAL_ROLLOUTS)
    hidden, back = hidden_ref[...], back_ref[...]
    total = squares(dot3(weighted(hidden, picked), grad), EVAL_ROLLOUTS)
    total = total + squares(dot3(weighted(back, picked), inp), EVAL_ROLLOUTS)
    scale = lax.rsqrt(total * (1.0 / K) + EPS)
    per_token = jnp.sum(picked * scale, axis=0, keepdims=True)
    tokens = x_ref.shape[0]
    base = 2 * tokens
    pack_ref[0, 0:tokens, :] = grad.astype(BF16)
    pack_ref[0, tokens:base, :] = inp.astype(BF16)
    pack_ref[0, base : base + RANK, 0:tokens] = (hidden * per_token).astype(BF16)
    pack_ref[0, base : base + RANK, tokens:base] = (back * per_token).astype(BF16)
    index = jnp.broadcast_to(index_ref[...].astype(F32), (RANK, tokens)).astype(BF16)
    pack_ref[0, base + RANK : base + 2 * RANK, 0:tokens] = index
    pack_ref[0, base + RANK : base + 2 * RANK, tokens:base] = index


def train_kernel(steps, size, side, place_ref, act_ref, factor_ref, index_ref, *rest):
    refs, rest = rest[: len(steps)], rest[len(steps) :]
    hi, lo = place_ref[0], place_ref[1]
    part = refs[0].shape[1] // 2
    held = rest[-1]
    for ref, (chunk, lows) in zip(refs, steps):
        for s, low in enumerate(lows):
            held[(hi ^ chunk) * size + (lo ^ low)] = ref[s, side * part : (side + 1) * part, :]
    width = held.shape[0] * part
    values = jnp.dot(act_ref[...], held[...].reshape(width, PW), preferred_element_type=F32)
    picked = one_hot(index_ref[...], TRAIN_EXAMPLES)
    raw = dot3(weighted(factor_ref[...], picked), values)
    total = squares(raw, TRAIN_EXAMPLES)
    if side == 0:
        rest[0][...] = raw
        rest[1][...] = total
        return
    raw_ref, total_ref, feats_ref = rest[:3]
    scale = lax.rsqrt((total_ref[...] + total) * (1.0 / K) + EPS)[None]
    shape = (RANK, TRAIN_EXAMPLES, PW)
    feats_ref[0] = (raw_ref[...].reshape(shape) * scale).reshape(RANK * TRAIN_EXAMPLES, PW).astype(BF16)
    feats_ref[1] = (raw.reshape(shape) * scale).reshape(RANK * TRAIN_EXAMPLES, PW).astype(BF16)


def make_tiles(steps, size, place_ref, feats_ref, refs, tiles_ref):
    hi, lo = place_ref[0], place_ref[1]
    tokens = refs[0].shape[1] // 2 - RANK
    base = 2 * tokens
    shape = (RANK, TRAIN_EXAMPLES, base)
    dot = functools.partial(lax.dot_general, dimension_numbers=NT, preferred_element_type=F32)
    for ref, (chunk, lows) in zip(refs, steps):
        for s in range(0, len(lows), 2):
            two = slice(s, s + 2)
            grad = ref[two, 0:tokens, :].reshape(base, PW)
            inp = ref[two, tokens:base, :].reshape(base, PW)
            coef = ref[two, base : base + RANK, :].astype(F32)
            hidden = jnp.concatenate([coef[0, :, 0:tokens], coef[1, :, 0:tokens]], axis=1)
            back = jnp.concatenate([coef[0, :, tokens:], coef[1, :, tokens:]], axis=1)
            mixed = jnp.sum(dot(feats_ref[0], grad).reshape(shape) * hidden[:, None, :], axis=0)
            mixed = mixed + jnp.sum(dot(feats_ref[1], inp).reshape(shape) * back[:, None, :], axis=0)
            high, low = split(mixed)
            for k in range(2):
                index = ref[s + k, base + RANK : base + 2 * RANK, 0:tokens].astype(F32)
                picked = one_hot(index[0:1].astype(jnp.int32), EVAL_ROLLOUTS).astype(BF16)
                lanes = slice(k * tokens, (k + 1) * tokens)
                tile = dot(picked, high[:, lanes]) + dot(picked, low[:, lanes])
                tiles_ref[(hi ^ chunk) * size + (lo ^ lows[s + k])] = tile


def tile_kernel(steps, size, place_ref, feats_ref, *rest):
    make_tiles(steps, size, place_ref, feats_ref, rest[: len(steps)], rest[len(steps)])


def score_kernel(steps, size, front, place_ref, chosen_ref, live_ref, feats_ref, *rest):
    refs, rest = rest[: len(steps)], rest[len(steps) :]
    out_ref, tiles = rest[-2:]
    make_tiles(steps, size, place_ref, feats_ref, refs, tiles)
    for chunk in range(front):
        for low in range(size):
            device = (place_ref[0] ^ chunk) * size + low
            tiles[device] = rest[0][device]
    for slot in range(SLOTS):
        factor = jnp.where(slot < live_ref[0], 1.0 / K**0.5, 0.0)
        out_ref[0, slot] = tiles[chosen_ref[slot]] * factor


def call(kernel, out_shape, scratch, flops, name, scalars, *arrays):
    return pl.pallas_call(
        kernel,
        out_shape=out_shape,
        in_specs=[SMEM] * len(scalars) + [VMEM] * len(arrays),
        out_specs=jax.tree.map(lambda _: VMEM, out_shape),
        scratch_shapes=scratch,
        compiler_params=pltpu.CompilerParams(vmem_limit_bytes=28 * 1024 * 1024),
        cost_estimate=pl.CostEstimate(flops=flops, bytes_accessed=4 * 2**20, transcendentals=0),
        name=name,
    )(*scalars, *arrays)


def per_device(
    n,
    train_layer_input,
    train_output_gradient,
    train_example_index,
    eval_layer_input,
    eval_output_gradient,
    eval_rollout_index,
    adapter_down,
    adapter_up,
    gradient_projector,
    input_projector,
    paired_eval_index,
    live_slot_count,
):
    place, size = placed(n)
    mine = lax.axis_index("train")
    tokens = eval_layer_input.shape[0]
    part = gradient_projector.shape[0]
    acts = (eval_layer_input, eval_output_gradient)
    sums = jax.ShapeDtypeStruct((2, tokens, PW), F32)
    tiles_shape = (n, EVAL_ROLLOUTS, TRAIN_EXAMPLES)

    def down(x):
        return lax.dot_general(adapter_down, x, (((0,), (1,)), ((), ())), preferred_element_type=F32)

    def up(g):
        return lax.dot_general(adapter_up, g, NT, preferred_element_type=F32)

    chosen = lax.dynamic_index_in_dim(paired_eval_index, mine, 0, keepdims=False)
    live = lax.dynamic_index_in_dim(live_slot_count, mine, 0, keepdims=True)
    early = (down(eval_layer_input), up(eval_output_gradient), chosen, live, train_layer_input, train_output_gradient)

    def middle(early):
        return down(early[4]), up(early[5])

    held = [pltpu.VMEM((2, 2, size, part, PW), BF16)]

    def begin(front, _):
        steps, arrays = plan(front, 0)
        kernel = functools.partial(begin_kernel, steps, size)
        return call(kernel, sums, held, 5 * 10**8, "eval_begin", [place], *acts, *arrays)

    block = jnp.concatenate([gradient_projector, input_projector], axis=0)[None]
    begun, back, early, middle = gather_chunks(block, n, early, middle, begin)
    front, extra = ([], []) if begun is None else (begun[1], [begun[0]])
    steps, arrays = plan(back, len(front))
    pack = call(
        functools.partial(eval_kernel, steps, size, len(extra)),
        jax.ShapeDtypeStruct((1, 2 * (tokens + RANK), PW), BF16),
        held,
        10**9,
        "eval_factors",
        [place],
        *acts,
        early[0],
        early[1],
        eval_rollout_index,
        *arrays,
        *extra,
    )
    steps, arrays = plan(front + back, 0)
    held = [pltpu.VMEM((n, part, PW), BF16)]
    rows = RANK * TRAIN_EXAMPLES
    raw = call(
        functools.partial(train_kernel, steps, size, 0),
        [jax.ShapeDtypeStruct((rows, PW), F32), jax.ShapeDtypeStruct((TRAIN_EXAMPLES, 1), F32)],
        held,
        2 * 10**9,
        "train_gradient_side",
        [place],
        train_output_gradient,
        middle[0],
        train_example_index,
        *arrays,
    )

    def finish_train(raw):
        return call(
            functools.partial(train_kernel, steps, size, 1),
            jax.ShapeDtypeStruct((2, rows, PW), BF16),
            held,
            2 * 10**9,
            "train_input_side",
            [place],
            train_layer_input,
            middle[1],
            train_example_index,
            *arrays,
            *raw,
        )

    def tile(front, feats):
        steps, arrays = plan(front, 0)
        kernel = functools.partial(tile_kernel, steps, size)
        shape = jax.ShapeDtypeStruct(tiles_shape, F32)
        return call(kernel, shape, [], 10**9, "front_tiles", [place], feats, *arrays)

    tiles, back, _, feats = gather_chunks(pack, n, raw, finish_train, tile)
    front, extra = ([], []) if tiles is None else (tiles[1], [tiles[0]])
    steps, arrays = plan(back, len(front))
    scores = call(
        functools.partial(score_kernel, steps, size, len(front)),
        jax.ShapeDtypeStruct((1, SLOTS, EVAL_ROLLOUTS, TRAIN_EXAMPLES), F32),
        [pltpu.VMEM(tiles_shape, F32)],
        10**9,
        "score_tiles",
        [place, early[2], early[3]],
        feats,
        *arrays,
        *extra,
    )
    return jnp.swapaxes(scores, 2, 3)


def solution(mesh):
    in_specs = (
        P(("parts", "train"), None),
        P(("parts", "train"), None),
        P(("parts", "train"), None),
        P(("parts", "train"), None),
        P(("parts", "train"), None),
        P(("parts", "train"), None),
        P(),
        P(),
        P("train", None),
        P("train", None),
        P("parts", None),
        P("parts"),
    )
    out_specs = P(("parts", "train"), None, None, None)
    return jax.shard_map(
        functools.partial(per_device, mesh.shape["train"]),
        mesh=mesh,
        in_specs=in_specs,
        out_specs=out_specs,
        check_vma=False,
    )
```

```python
import functools

import jax
import jax.numpy as jnp
from jax import lax
from jax.experimental import pallas as pl
from jax.experimental.pallas import tpu as pltpu
from jax.sharding import PartitionSpec as P

RANK = 16
PW = 256
K = 2 * RANK * PW
TRAIN_EXAMPLES = 32
EVAL_ROLLOUTS = 16
SLOTS = 16
EPS = 1e-06

VMEM = pl.BlockSpec(memory_space=pltpu.VMEM)
SMEM = pl.BlockSpec(memory_space=pltpu.SMEM)
BF16 = jnp.bfloat16
F32 = jnp.float32
NT = (((1,), (1,)), ((), ()))


def gather_blocks(block, n, early, middle, third, late):
    if n != 32:
        whole = lax.all_gather(block, "train", axis=0, tiled=True)
        middle = middle(early)
        return None, [], [(whole, 0, list(range(n)))], early, middle, third(middle)

    def permute(held, mask):
        return lax.ppermute(held, "train", [(i, i ^ mask) for i in range(n)])

    def join(chunk):
        return jnp.concatenate([rows[chunk], first[chunk]], axis=0)

    def near(chunk):
        one, two = orders[chunk]
        return [(held[chunk], chunk, [0, one]), (swapped[chunk], chunk, [1, one ^ 1])]

    def far(chunk):
        one, two = orders[chunk]
        got = second[chunk]
        return [(got, chunk, [two, one ^ two]), (permute(got, 1), chunk, [two ^ 1, one ^ two ^ 1])]

    orders = [(2, 4), (4, 2), (2, 4), (4, 2)]
    rows = [block] + [permute(block, mask) for mask in (8, 16, 24)]
    first, held, second, swapped = [permute(block, 2)], [], [], []
    first[0], rows[1], early = lax.optimization_barrier((first[0], rows[1], early))
    held.append(join(0))
    held[0], early = lax.optimization_barrier((held[0], early))
    first.append(permute(rows[1], orders[1][0]))
    second.append(permute(held[0], orders[0][1]))
    swapped.append(permute(held[0], 1))
    middle = middle(early)
    rows[2], rows[3], first[1], middle = lax.optimization_barrier((rows[2], rows[3], first[1], middle))
    first.append(permute(rows[2], orders[2][0]))
    first.append(permute(rows[3], orders[3][0]))
    held.append(join(1))
    second.append(permute(held[1], orders[1][1]))
    swapped.append(permute(held[1], 1))
    third = third(middle)
    first[2], first[3], second[0], third = lax.optimization_barrier((first[2], first[3], second[0], third))
    for chunk in (2, 3):
        held.append(join(chunk))
        second.append(permute(held[chunk], orders[chunk][1]))
        swapped.append(permute(held[chunk], 1))
    front = near(0) + far(0) + near(1) + far(1) + near(2) + near(3)
    done = late(front, third)
    second[2], second[3], done = lax.optimization_barrier((second[2], second[3], done))
    return done, front, far(2) + far(3), early, middle, third


def placed(n):
    mine = lax.axis_index("train").astype(jnp.int32)
    if n != 32:
        return jnp.stack([mine * 0, mine * 0, mine]), n
    return jnp.stack([mine // 8, mine % 8, mine]), 8


def plan(entries):
    return [(chunk, lows) for _, chunk, lows in entries], [array for array, _, _ in entries]


def split(value):
    high = value.astype(BF16)
    return high, (value - high.astype(F32)).astype(BF16)


def dot3(left, right):
    lh, ll = split(left)
    rh, rl = split(right)
    dot = functools.partial(jnp.dot, preferred_element_type=F32)
    return dot(lh, rh) + (dot(lh, rl) + dot(ll, rh))


def one_hot(index_row, count):
    steps = lax.broadcasted_iota(jnp.int32, (count, index_row.shape[1]), 0)
    return (index_row == steps).astype(F32)


def weighted(rows, picked):
    ranks, tokens = rows.shape
    return (rows[:, None, :] * picked[None, :, :]).reshape(ranks * picked.shape[0], tokens)


def squares(raw, items):
    each = jnp.sum(raw * raw, axis=1, keepdims=True)
    return jnp.sum(each.reshape(RANK, items, 1), axis=0)


def pairs_of(steps):
    pairs = {}
    for k, (chunk, lows) in enumerate(steps):
        for s, low in enumerate(lows):
            pairs.setdefault((chunk, low // 2), []).append((k, s, low))
    return pairs


def project(steps, size, place_ref, x_ref, g_ref, refs, held, grad, inp):
    hi, lo = place_ref[0], place_ref[1]
    part = refs[0].shape[1] // 2
    pairs = pairs_of(steps)
    for p, places in enumerate(pairs.values()):
        for k, s, low in places:
            held[p, 0, (lo ^ low) & 1] = refs[k][s, 0:part, :]
            held[p, 1, (lo ^ low) & 1] = refs[k][s, part : 2 * part, :]
    width = 2 * part
    for p, ((chunk, _), places) in enumerate(pairs.items()):
        device = (hi ^ chunk) * size + ((lo ^ places[0][2]) & -2)
        columns = pl.ds(pl.multiple_of(device * part, width), width)
        more = jnp.dot(g_ref[:, columns], held[p, 0].reshape(width, PW), preferred_element_type=F32)
        grad = more if grad is None else grad + more
        more = jnp.dot(x_ref[:, columns], held[p, 1].reshape(width, PW), preferred_element_type=F32)
        inp = more if inp is None else inp + more
    return grad, inp


def begin_kernel(steps, size, place_ref, x_ref, g_ref, *rest):
    refs, (sums_ref, held) = rest[: len(steps)], rest[len(steps) :]
    grad, inp = project(steps, size, place_ref, x_ref, g_ref, refs, held, None, None)
    sums_ref[0] = grad
    sums_ref[1] = inp


def eval_kernel(steps, size, begun, place_ref, x_ref, g_ref, hidden_ref, back_ref, index_ref, *rest):
    refs, rest = rest[: len(steps)], rest[len(steps) :]
    pack_ref, held = rest[begun:]
    grad, inp = (rest[0][0], rest[0][1]) if begun else (None, None)
    grad, inp = project(steps, size, place_ref, x_ref, g_ref, refs, held, grad, inp)
    picked = one_hot(index_ref[...], EVAL_ROLLOUTS)
    hidden, back = hidden_ref[...], back_ref[...]
    total = squares(dot3(weighted(hidden, picked), grad), EVAL_ROLLOUTS)
    total = total + squares(dot3(weighted(back, picked), inp), EVAL_ROLLOUTS)
    scale = lax.rsqrt(total * (1.0 / K) + EPS)
    per_token = jnp.sum(picked * scale, axis=0, keepdims=True)
    tokens = x_ref.shape[0]
    base = 2 * tokens
    pack_ref[0, 0:tokens, :] = grad.astype(BF16)
    pack_ref[0, tokens:base, :] = inp.astype(BF16)
    pack_ref[0, base : base + RANK, 0:tokens] = (hidden * per_token).astype(BF16)
    pack_ref[0, base : base + RANK, tokens:base] = (back * per_token).astype(BF16)
    index = jnp.broadcast_to(index_ref[...].astype(F32), (RANK, tokens)).astype(BF16)
    pack_ref[0, base + RANK : base + 2 * RANK, 0:tokens] = index
    pack_ref[0, base + RANK : base + 2 * RANK, tokens:base] = index


def train_kernel(steps, size, side, place_ref, act_ref, adapter_ref, *rest):
    refs, rest = rest[: len(steps)], rest[len(steps) :]
    hi, lo = place_ref[0], place_ref[1]
    part = refs[0].shape[1] // 2
    held = rest[-1]
    for ref, (chunk, lows) in zip(refs, steps):
        for s, low in enumerate(lows):
            held[(hi ^ chunk) * size + (lo ^ low)] = ref[s, side * part : (side + 1) * part, :]
    width = held.shape[0] * part
    factor = lax.dot_general(adapter_ref[...], act_ref[...], NT, preferred_element_type=F32)
    values = jnp.dot(act_ref[...], held[...].reshape(width, PW), preferred_element_type=F32)
    if side == 0:
        values_ref, factor_ref = rest[:2]
        values_ref[...] = values
        factor_ref[...] = factor
        return
    back_ref, index_ref, raw_ref, total_ref, factor_ref = rest[:5]
    picked = one_hot(index_ref[...], TRAIN_EXAMPLES)
    raw = dot3(weighted(back_ref[...], picked), values)
    raw_ref[...] = raw
    total_ref[...] = squares(raw, TRAIN_EXAMPLES)
    factor_ref[...] = factor


def feats_kernel(hidden_ref, values_ref, raw_ref, total_ref, index_ref, feats_ref):
    picked = one_hot(index_ref[...], TRAIN_EXAMPLES)
    raw = dot3(weighted(hidden_ref[...], picked), values_ref[...])
    total = total_ref[...] + squares(raw, TRAIN_EXAMPLES)
    scale = lax.rsqrt(total * (1.0 / K) + EPS)[None]
    shape = (RANK, TRAIN_EXAMPLES, PW)
    feats_ref[0] = (raw.reshape(shape) * scale).reshape(RANK * TRAIN_EXAMPLES, PW).astype(BF16)
    feats_ref[1] = (raw_ref[...].reshape(shape) * scale).reshape(RANK * TRAIN_EXAMPLES, PW).astype(BF16)


def make_tiles(steps, size, place_ref, feats_ref, refs, tiles_ref):
    hi, lo = place_ref[0], place_ref[1]
    tokens = refs[0].shape[1] // 2 - RANK
    base = 2 * tokens
    shape = (RANK, TRAIN_EXAMPLES, base)
    dot = functools.partial(lax.dot_general, dimension_numbers=NT, preferred_element_type=F32)
    for ref, (chunk, lows) in zip(refs, steps):
        for s in range(0, len(lows), 2):
            two = slice(s, s + 2)
            grad = ref[two, 0:tokens, :].reshape(base, PW)
            inp = ref[two, tokens:base, :].reshape(base, PW)
            coef = ref[two, base : base + RANK, :].astype(F32)
            hidden = jnp.concatenate([coef[0, :, 0:tokens], coef[1, :, 0:tokens]], axis=1)
            back = jnp.concatenate([coef[0, :, tokens:], coef[1, :, tokens:]], axis=1)
            mixed = jnp.sum(dot(feats_ref[0], grad).reshape(shape) * hidden[:, None, :], axis=0)
            mixed = mixed + jnp.sum(dot(feats_ref[1], inp).reshape(shape) * back[:, None, :], axis=0)
            high, low = split(mixed)
            for k in range(2):
                index = ref[s + k, base + RANK : base + 2 * RANK, 0:tokens].astype(F32)
                picked = one_hot(index[0:1].astype(jnp.int32), EVAL_ROLLOUTS).astype(BF16)
                lanes = slice(k * tokens, (k + 1) * tokens)
                tile = dot(picked, high[:, lanes]) + dot(picked, low[:, lanes])
                tiles_ref[(hi ^ chunk) * size + (lo ^ lows[s + k])] = tile


def tile_kernel(steps, size, place_ref, feats_ref, *rest):
    make_tiles(steps, size, place_ref, feats_ref, rest[: len(steps)], rest[len(steps)])


def score_kernel(steps, front, size, place_ref, pairing_ref, live_ref, feats_ref, *rest):
    refs, rest = rest[: len(steps)], rest[len(steps) :]
    out_ref, tiles = rest[-2:]
    hi, lo, mine = place_ref[0], place_ref[1], place_ref[2]
    make_tiles(steps, size, place_ref, feats_ref, refs, tiles)
    for chunk, lows in front:
        for low in lows:
            device = (hi ^ chunk) * size + (lo ^ low)
            tiles[device] = rest[0][device]
    for slot in range(SLOTS):
        factor = jnp.where(slot < live_ref[mine], 1.0 / K**0.5, 0.0)
        out_ref[0, slot] = tiles[pairing_ref[slot, mine]] * factor


def call(kernel, out_shape, scratch, flops, name, scalars, *arrays):
    return pl.pallas_call(
        kernel,
        out_shape=out_shape,
        in_specs=[SMEM] * len(scalars) + [VMEM] * len(arrays),
        out_specs=jax.tree.map(lambda _: VMEM, out_shape),
        scratch_shapes=scratch,
        compiler_params=pltpu.CompilerParams(vmem_limit_bytes=28 * 1024 * 1024),
        cost_estimate=pl.CostEstimate(flops=flops, bytes_accessed=4 * 2**20, transcendentals=0),
        name=name,
    )(*scalars, *arrays)


def per_device(
    n,
    train_layer_input,
    train_output_gradient,
    train_example_index,
    eval_layer_input,
    eval_output_gradient,
    eval_rollout_index,
    adapter_down,
    adapter_up,
    gradient_projector,
    input_projector,
    paired_eval_index,
    live_slot_count,
):
    place, size = placed(n)
    tokens = eval_layer_input.shape[0]
    part = gradient_projector.shape[0]
    acts = (eval_layer_input, eval_output_gradient)
    sums = jax.ShapeDtypeStruct((2, tokens, PW), F32)
    tiles_shape = (n, EVAL_ROLLOUTS, TRAIN_EXAMPLES)

    def down(x):
        return lax.dot_general(adapter_down, x, (((0,), (1,)), ((), ())), preferred_element_type=F32)

    def up(g):
        return lax.dot_general(adapter_up, g, NT, preferred_element_type=F32)

    def room(steps):
        return [pltpu.VMEM((len(pairs_of(steps)), 2, 2, part, PW), BF16)]

    def begin(front, early):
        steps, arrays = plan(front)
        place = early[2]
        kernel = functools.partial(begin_kernel, steps, size)
        return call(kernel, sums, room(steps), 8 * 10**8, "eval_begin", [place], *acts, *arrays)

    early = (down(eval_layer_input), up(eval_output_gradient), place)
    block = jnp.concatenate([gradient_projector, input_projector], axis=0)[None]
    begun, front, back, early, _, _ = gather_blocks(block, n, early, tuple, tuple, begin)
    place = early[2]
    steps, arrays = plan(back)
    extra = [] if begun is None else [begun]
    pack = call(
        functools.partial(eval_kernel, steps, size, len(extra)),
        jax.ShapeDtypeStruct((1, 2 * (tokens + RANK), PW), BF16),
        room(steps),
        10**9,
        "eval_factors",
        [place],
        *acts,
        early[0],
        early[1],
        eval_rollout_index,
        *arrays,
        *extra,
    )
    every, everything = plan(front + back)
    held = [pltpu.VMEM((n, part, PW), BF16)]
    rows = RANK * TRAIN_EXAMPLES
    values_shape = jax.ShapeDtypeStruct((train_layer_input.shape[0], PW), F32)
    factor_shape = jax.ShapeDtypeStruct((RANK, train_layer_input.shape[0]), F32)
    gradient_side = call(
        functools.partial(train_kernel, every, size, 0),
        [values_shape, factor_shape],
        held,
        2 * 10**9,
        "train_gradient_side",
        [place],
        train_output_gradient,
        adapter_up,
        *everything,
    )

    def input_side(gradient_side):
        values, back = gradient_side
        raw, total, hidden = call(
            functools.partial(train_kernel, every, size, 1),
            [jax.ShapeDtypeStruct((rows, PW), F32), jax.ShapeDtypeStruct((TRAIN_EXAMPLES, 1), F32), factor_shape],
            held,
            2 * 10**9,
            "train_input_side",
            [place],
            train_layer_input,
            adapter_down.T,
            *everything,
            back,
            train_example_index,
        )
        return hidden, values, raw, total

    def features(sides):
        shape = jax.ShapeDtypeStruct((2, rows, PW), BF16)
        return call(feats_kernel, shape, [], 10**9, "train_features", [], *sides, train_example_index)

    def tile(front, feats):
        steps, arrays = plan(front)
        kernel = functools.partial(tile_kernel, steps, size)
        return call(kernel, jax.ShapeDtypeStruct(tiles_shape, F32), [], 10**9, "front_tiles", [place], feats, *arrays)

    tiles, front, back, _, _, feats = gather_blocks(pack, n, gradient_side, input_side, features, tile)
    steps, arrays = plan(back)
    scores = call(
        functools.partial(score_kernel, steps, plan(front)[0], size),
        jax.ShapeDtypeStruct((1, SLOTS, EVAL_ROLLOUTS, TRAIN_EXAMPLES), F32),
        [pltpu.VMEM(tiles_shape, F32)],
        10**9,
        "score_tiles",
        [place, paired_eval_index.T, live_slot_count],
        feats,
        *arrays,
        *([] if tiles is None else [tiles]),
    )
    return jnp.swapaxes(scores, 2, 3)


def solution(mesh):
    in_specs = (
        P(("parts", "train"), None),
        P(("parts", "train"), None),
        P(("parts", "train"), None),
        P(("parts", "train"), None),
        P(("parts", "train"), None),
        P(("parts", "train"), None),
        P(),
        P(),
        P("train", None),
        P("train", None),
        P("parts", None),
        P("parts"),
    )
    out_specs = P(("parts", "train"), None, None, None)
    return jax.shard_map(
        functools.partial(per_device, mesh.shape["train"]),
        mesh=mesh,
        in_specs=in_specs,
        out_specs=out_specs,
        check_vma=False,
    )
```

```python
import functools

import jax
import jax.numpy as jnp
from jax import lax
from jax.experimental import pallas as pl
from jax.experimental.pallas import tpu as pltpu
from jax.sharding import PartitionSpec as P

RANK = 16
PW = 256
K = 2 * RANK * PW
TRAIN_EXAMPLES = 32
EVAL_ROLLOUTS = 16
SLOTS = 16
EPS = 1e-06

VMEM = pl.BlockSpec(memory_space=pltpu.VMEM)
SMEM = pl.BlockSpec(memory_space=pltpu.SMEM)
BF16 = jnp.bfloat16
F32 = jnp.float32
NT = (((1,), (1,)), ((), ()))


def gather_blocks(block, n, early, middle, third, late):
    if n != 32:
        whole = lax.all_gather(block, "train", axis=0, tiled=True)
        middle = middle(early)
        return None, [], [(whole, 0, list(range(n)))], early, middle, third(middle)

    def permute(held, mask):
        return lax.ppermute(held, "train", [(i, i ^ mask) for i in range(n)])

    def join(chunk):
        return jnp.concatenate([rows[chunk], first[chunk]], axis=0)

    def near(chunk):
        one, two = orders[chunk]
        return [(held[chunk], chunk, [0, one]), (swapped[chunk], chunk, [1, one ^ 1])]

    def far(chunk):
        one, two = orders[chunk]
        got = second[chunk]
        return [(got, chunk, [two, one ^ two]), (permute(got, 1), chunk, [two ^ 1, one ^ two ^ 1])]

    orders = [(2, 4), (4, 2), (2, 4), (4, 2)]
    rows = [block] + [permute(block, mask) for mask in (8, 16, 24)]
    first, held, second, swapped = [permute(block, 2)], [], [], []
    first[0], rows[1], early = lax.optimization_barrier((first[0], rows[1], early))
    held.append(join(0))
    held[0], early = lax.optimization_barrier((held[0], early))
    first.append(permute(rows[1], orders[1][0]))
    second.append(permute(held[0], orders[0][1]))
    swapped.append(permute(held[0], 1))
    middle = middle(early)
    rows[2], rows[3], first[1], middle = lax.optimization_barrier((rows[2], rows[3], first[1], middle))
    first.append(permute(rows[2], orders[2][0]))
    first.append(permute(rows[3], orders[3][0]))
    held.append(join(1))
    second.append(permute(held[1], orders[1][1]))
    swapped.append(permute(held[1], 1))
    third = third(middle)
    first[2], first[3], second[0], third = lax.optimization_barrier((first[2], first[3], second[0], third))
    for chunk in (2, 3):
        held.append(join(chunk))
        second.append(permute(held[chunk], orders[chunk][1]))
        swapped.append(permute(held[chunk], 1))
    second[1] = lax.optimization_barrier((second[1], held[2], held[3]))[0]
    front = near(0) + far(0) + near(1) + far(1) + near(2) + near(3)
    done = late(front, third)
    second[2], second[3], done = lax.optimization_barrier((second[2], second[3], done))
    return done, front, far(2) + far(3), early, middle, third


def placed(n):
    mine = lax.axis_index("train").astype(jnp.int32)
    if n != 32:
        return jnp.stack([mine * 0, mine * 0, mine]), n
    return jnp.stack([mine // 8, mine % 8, mine]), 8


def plan(entries):
    return [(chunk, lows) for _, chunk, lows in entries], [array for array, _, _ in entries]


def split(value):
    high = value.astype(BF16)
    return high, (value - high.astype(F32)).astype(BF16)


def dot3(left, right):
    lh, ll = split(left)
    rh, rl = split(right)
    dot = functools.partial(jnp.dot, preferred_element_type=F32)
    return dot(lh, rh) + (dot(lh, rl) + dot(ll, rh))


def one_hot(index_row, count):
    steps = lax.broadcasted_iota(jnp.int32, (count, index_row.shape[1]), 0)
    return (index_row == steps).astype(F32)


def weighted(rows, picked):
    ranks, tokens = rows.shape
    return (rows[:, None, :] * picked[None, :, :]).reshape(ranks * picked.shape[0], tokens)


def squares(raw, items):
    each = jnp.sum(raw * raw, axis=1, keepdims=True)
    return jnp.sum(each.reshape(RANK, items, 1), axis=0)


def pairs_of(steps):
    pairs = {}
    for k, (chunk, lows) in enumerate(steps):
        for s, low in enumerate(lows):
            pairs.setdefault((chunk, low // 2), []).append((k, s, low))
    return pairs


def project(steps, size, place_ref, x_ref, g_ref, refs, held, grad, inp):
    hi, lo = place_ref[0], place_ref[1]
    part = refs[0].shape[1] // 2
    pairs = pairs_of(steps)
    for p, places in enumerate(pairs.values()):
        for k, s, low in places:
            held[p, 0, (lo ^ low) & 1] = refs[k][s, 0:part, :]
            held[p, 1, (lo ^ low) & 1] = refs[k][s, part : 2 * part, :]
    width = 2 * part
    for p, ((chunk, _), places) in enumerate(pairs.items()):
        device = (hi ^ chunk) * size + ((lo ^ places[0][2]) & -2)
        columns = pl.ds(pl.multiple_of(device * part, width), width)
        more = jnp.dot(g_ref[:, columns], held[p, 0].reshape(width, PW), preferred_element_type=F32)
        grad = more if grad is None else grad + more
        more = jnp.dot(x_ref[:, columns], held[p, 1].reshape(width, PW), preferred_element_type=F32)
        inp = more if inp is None else inp + more
    return grad, inp


def begin_kernel(steps, size, place_ref, x_ref, g_ref, *rest):
    refs, (sums_ref, held) = rest[: len(steps)], rest[len(steps) :]
    grad, inp = project(steps, size, place_ref, x_ref, g_ref, refs, held, None, None)
    sums_ref[0] = grad
    sums_ref[1] = inp


def eval_kernel(steps, size, begun, place_ref, x_ref, g_ref, hidden_ref, back_ref, index_ref, *rest):
    refs, rest = rest[: len(steps)], rest[len(steps) :]
    pack_ref, held = rest[begun:]
    grad, inp = (rest[0][0], rest[0][1]) if begun else (None, None)
    grad, inp = project(steps, size, place_ref, x_ref, g_ref, refs, held, grad, inp)
    picked = one_hot(index_ref[...], EVAL_ROLLOUTS)
    hidden, back = hidden_ref[...], back_ref[...]
    total = squares(dot3(weighted(hidden, picked), grad), EVAL_ROLLOUTS)
    total = total + squares(dot3(weighted(back, picked), inp), EVAL_ROLLOUTS)
    scale = lax.rsqrt(total * (1.0 / K) + EPS)
    per_token = jnp.sum(picked * scale, axis=0, keepdims=True)
    tokens = x_ref.shape[0]
    base = 2 * tokens
    pack_ref[0, 0:tokens, :] = grad.astype(BF16)
    pack_ref[0, tokens:base, :] = inp.astype(BF16)
    pack_ref[0, base : base + RANK, 0:tokens] = (hidden * per_token).astype(BF16)
    pack_ref[0, base : base + RANK, tokens:base] = (back * per_token).astype(BF16)
    index = jnp.broadcast_to(index_ref[...].astype(F32), (RANK, tokens)).astype(BF16)
    pack_ref[0, base + RANK : base + 2 * RANK, 0:tokens] = index
    pack_ref[0, base + RANK : base + 2 * RANK, tokens:base] = index


def train_kernel(steps, size, side, place_ref, act_ref, adapter_ref, *rest):
    refs, rest = rest[: len(steps)], rest[len(steps) :]
    hi, lo = place_ref[0], place_ref[1]
    part = refs[0].shape[1] // 2
    held = rest[-1]
    for ref, (chunk, lows) in zip(refs, steps):
        for s, low in enumerate(lows):
            held[(hi ^ chunk) * size + (lo ^ low)] = ref[s, side * part : (side + 1) * part, :]
    width = held.shape[0] * part
    factor = lax.dot_general(adapter_ref[...], act_ref[...], NT, preferred_element_type=F32)
    values = jnp.dot(act_ref[...], held[...].reshape(width, PW), preferred_element_type=F32)
    if side == 0:
        values_ref, factor_ref = rest[:2]
        values_ref[...] = values
        factor_ref[...] = factor
        return
    back_ref, index_ref, raw_ref, total_ref, factor_ref = rest[:5]
    picked = one_hot(index_ref[...], TRAIN_EXAMPLES)
    raw = dot3(weighted(back_ref[...], picked), values)
    raw_ref[...] = raw
    total_ref[...] = squares(raw, TRAIN_EXAMPLES)
    factor_ref[...] = factor


def feats_kernel(hidden_ref, values_ref, raw_ref, total_ref, index_ref, feats_ref):
    picked = one_hot(index_ref[...], TRAIN_EXAMPLES)
    raw = dot3(weighted(hidden_ref[...], picked), values_ref[...])
    total = total_ref[...] + squares(raw, TRAIN_EXAMPLES)
    scale = lax.rsqrt(total * (1.0 / K) + EPS)[None]
    shape = (RANK, TRAIN_EXAMPLES, PW)
    feats_ref[0] = (raw.reshape(shape) * scale).reshape(RANK * TRAIN_EXAMPLES, PW).astype(BF16)
    feats_ref[1] = (raw_ref[...].reshape(shape) * scale).reshape(RANK * TRAIN_EXAMPLES, PW).astype(BF16)


def make_tiles(steps, size, place_ref, feats_ref, refs, tiles_ref):
    hi, lo = place_ref[0], place_ref[1]
    tokens = refs[0].shape[1] // 2 - RANK
    base = 2 * tokens
    shape = (RANK, TRAIN_EXAMPLES, base)
    dot = functools.partial(lax.dot_general, dimension_numbers=NT, preferred_element_type=F32)
    for ref, (chunk, lows) in zip(refs, steps):
        for s in range(0, len(lows), 2):
            two = slice(s, s + 2)
            grad = ref[two, 0:tokens, :].reshape(base, PW)
            inp = ref[two, tokens:base, :].reshape(base, PW)
            coef = ref[two, base : base + RANK, :].astype(F32)
            hidden = jnp.concatenate([coef[0, :, 0:tokens], coef[1, :, 0:tokens]], axis=1)
            back = jnp.concatenate([coef[0, :, tokens:], coef[1, :, tokens:]], axis=1)
            mixed = jnp.sum(dot(feats_ref[0], grad).reshape(shape) * hidden[:, None, :], axis=0)
            mixed = mixed + jnp.sum(dot(feats_ref[1], inp).reshape(shape) * back[:, None, :], axis=0)
            high, low = split(mixed)
            for k in range(2):
                index = ref[s + k, base + RANK : base + 2 * RANK, 0:tokens].astype(F32)
                picked = one_hot(index[0:1].astype(jnp.int32), EVAL_ROLLOUTS).astype(BF16)
                lanes = slice(k * tokens, (k + 1) * tokens)
                tile = dot(picked, high[:, lanes]) + dot(picked, low[:, lanes])
                tiles_ref[(hi ^ chunk) * size + (lo ^ lows[s + k])] = tile


def tile_kernel(steps, size, place_ref, feats_ref, *rest):
    make_tiles(steps, size, place_ref, feats_ref, rest[: len(steps)], rest[len(steps)])


def score_kernel(steps, front, size, place_ref, pairing_ref, live_ref, feats_ref, *rest):
    refs, rest = rest[: len(steps)], rest[len(steps) :]
    out_ref, tiles = rest[-2:]
    hi, lo, mine = place_ref[0], place_ref[1], place_ref[2]
    make_tiles(steps, size, place_ref, feats_ref, refs, tiles)
    for chunk, lows in front:
        for low in lows:
            device = (hi ^ chunk) * size + (lo ^ low)
            tiles[device] = rest[0][device]
    for slot in range(SLOTS):
        factor = jnp.where(slot < live_ref[mine], 1.0 / K**0.5, 0.0)
        out_ref[0, slot] = tiles[pairing_ref[slot, mine]] * factor


def call(kernel, out_shape, scratch, flops, name, scalars, *arrays):
    return pl.pallas_call(
        kernel,
        out_shape=out_shape,
        in_specs=[SMEM] * len(scalars) + [VMEM] * len(arrays),
        out_specs=jax.tree.map(lambda _: VMEM, out_shape),
        scratch_shapes=scratch,
        compiler_params=pltpu.CompilerParams(vmem_limit_bytes=28 * 1024 * 1024),
        cost_estimate=pl.CostEstimate(flops=flops // 1000, bytes_accessed=4096, transcendentals=0),
        name=name,
    )(*scalars, *arrays)


def per_device(
    n,
    train_layer_input,
    train_output_gradient,
    train_example_index,
    eval_layer_input,
    eval_output_gradient,
    eval_rollout_index,
    adapter_down,
    adapter_up,
    gradient_projector,
    input_projector,
    paired_eval_index,
    live_slot_count,
):
    place, size = placed(n)
    tokens = eval_layer_input.shape[0]
    part = gradient_projector.shape[0]
    acts = (eval_layer_input, eval_output_gradient)
    sums = jax.ShapeDtypeStruct((2, tokens, PW), F32)
    tiles_shape = (n, EVAL_ROLLOUTS, TRAIN_EXAMPLES)

    def down(x):
        return lax.dot_general(adapter_down, x, (((0,), (1,)), ((), ())), preferred_element_type=F32)

    def up(g):
        return lax.dot_general(adapter_up, g, NT, preferred_element_type=F32)

    def room(steps):
        return [pltpu.VMEM((len(pairs_of(steps)), 2, 2, part, PW), BF16)]

    def begin(front, early):
        steps, arrays = plan(front)
        place = early[2]
        kernel = functools.partial(begin_kernel, steps, size)
        return call(kernel, sums, room(steps), 8 * 10**8, "eval_begin", [place], *acts, *arrays)

    early = (down(eval_layer_input), up(eval_output_gradient), place)
    block = jnp.concatenate([gradient_projector, input_projector], axis=0)[None]
    begun, front, back, early, _, _ = gather_blocks(block, n, early, tuple, tuple, begin)
    place = early[2]
    steps, arrays = plan(back)
    extra = [] if begun is None else [begun]
    pack = call(
        functools.partial(eval_kernel, steps, size, len(extra)),
        jax.ShapeDtypeStruct((1, 2 * (tokens + RANK), PW), BF16),
        room(steps),
        10**9,
        "eval_factors",
        [place],
        *acts,
        early[0],
        early[1],
        eval_rollout_index,
        *arrays,
        *extra,
    )
    every, everything = plan(front + back)
    held = [pltpu.VMEM((n, part, PW), BF16)]
    rows = RANK * TRAIN_EXAMPLES
    values_shape = jax.ShapeDtypeStruct((train_layer_input.shape[0], PW), F32)
    factor_shape = jax.ShapeDtypeStruct((RANK, train_layer_input.shape[0]), F32)

    def gradient_side(early):
        return call(
            functools.partial(train_kernel, every, size, 0),
            [values_shape, factor_shape],
            held,
            2 * 10**9,
            "train_gradient_side",
            [early[0]],
            train_output_gradient,
            adapter_up,
            *everything,
        )

    def input_side(gradient_side):
        values, back = gradient_side
        raw, total, hidden = call(
            functools.partial(train_kernel, every, size, 1),
            [jax.ShapeDtypeStruct((rows, PW), F32), jax.ShapeDtypeStruct((TRAIN_EXAMPLES, 1), F32), factor_shape],
            held,
            2 * 10**9,
            "train_input_side",
            [place],
            train_layer_input,
            adapter_down.T,
            *everything,
            back,
            train_example_index,
        )
        return hidden, values, raw, total

    def features(gradient_side):
        shape = jax.ShapeDtypeStruct((2, rows, PW), BF16)
        sides = input_side(gradient_side)
        return call(feats_kernel, shape, [], 10**9, "train_features", [], *sides, train_example_index)

    def tile(front, feats):
        steps, arrays = plan(front)
        kernel = functools.partial(tile_kernel, steps, size)
        return call(kernel, jax.ShapeDtypeStruct(tiles_shape, F32), [], 10**9, "front_tiles", [place], feats, *arrays)

    tiles, front, back, _, _, feats = gather_blocks(pack, n, (place,), gradient_side, features, tile)
    steps, arrays = plan(back)
    scores = call(
        functools.partial(score_kernel, steps, plan(front)[0], size),
        jax.ShapeDtypeStruct((1, SLOTS, EVAL_ROLLOUTS, TRAIN_EXAMPLES), F32),
        [pltpu.VMEM(tiles_shape, F32)],
        10**9,
        "score_tiles",
        [place, paired_eval_index.T, live_slot_count],
        feats,
        *arrays,
        *([] if tiles is None else [tiles]),
    )
    return jnp.swapaxes(scores, 2, 3)


def solution(mesh):
    in_specs = (
        P(("parts", "train"), None),
        P(("parts", "train"), None),
        P(("parts", "train"), None),
        P(("parts", "train"), None),
        P(("parts", "train"), None),
        P(("parts", "train"), None),
        P(),
        P(),
        P("train", None),
        P("train", None),
        P("parts", None),
        P("parts"),
    )
    out_specs = P(("parts", "train"), None, None, None)
    return jax.shard_map(
        functools.partial(per_device, mesh.shape["train"]),
        mesh=mesh,
        in_specs=in_specs,
        out_specs=out_specs,
        check_vma=False,
    )
```

```python
import functools

import jax
import jax.numpy as jnp
from jax import lax
from jax.experimental import pallas as pl
from jax.experimental.pallas import tpu as pltpu
from jax.sharding import PartitionSpec as P

RANK = 16
PW = 256
K = 2 * RANK * PW
TRAIN_EXAMPLES = 32
EVAL_ROLLOUTS = 16
SLOTS = 16
EPS = 1e-06

VMEM = pl.BlockSpec(memory_space=pltpu.VMEM)
SMEM = pl.BlockSpec(memory_space=pltpu.SMEM)
BF16 = jnp.bfloat16
F32 = jnp.float32
NT = (((1,), (1,)), ((), ()))


def gather_blocks(block, n, early, middle, third, late):
    if n != 32:
        whole = lax.all_gather(block, "train", axis=0, tiled=True)
        middle = middle(early)
        return None, [], [(whole, 0, list(range(n)))], early, middle, third(middle)

    def permute(held, mask):
        return lax.ppermute(held, "train", [(i, i ^ mask) for i in range(n)])

    def join(chunk):
        return jnp.concatenate([rows[chunk], first[chunk]], axis=0)

    def near(chunk):
        one, two = orders[chunk]
        return [(held[chunk], chunk, [0, one]), (swapped[chunk], chunk, [1, one ^ 1])]

    def far(chunk):
        one, two = orders[chunk]
        got = second[chunk]
        return [(got, chunk, [two, one ^ two]), (permute(got, 1), chunk, [two ^ 1, one ^ two ^ 1])]

    orders = [(2, 4), (4, 2), (2, 4), (4, 2)]
    rows = [block] + [permute(block, mask) for mask in (8, 16, 24)]
    first, held, second, swapped = [permute(block, 2)], [], [], []
    first[0], rows[1], early = lax.optimization_barrier((first[0], rows[1], early))
    held.append(join(0))
    held[0], early = lax.optimization_barrier((held[0], early))
    first.append(permute(rows[1], orders[1][0]))
    second.append(permute(held[0], orders[0][1]))
    swapped.append(permute(held[0], 1))
    middle = middle(early)
    rows[2], rows[3], first[1], middle = lax.optimization_barrier((rows[2], rows[3], first[1], middle))
    first.append(permute(rows[2], orders[2][0]))
    first.append(permute(rows[3], orders[3][0]))
    held.append(join(1))
    second.append(permute(held[1], orders[1][1]))
    swapped.append(permute(held[1], 1))
    third = third(middle)
    first[2], first[3], second[0], third = lax.optimization_barrier((first[2], first[3], second[0], third))
    for chunk in (2, 3):
        held.append(join(chunk))
        second.append(permute(held[chunk], orders[chunk][1]))
        swapped.append(permute(held[chunk], 1))
    second[1] = lax.optimization_barrier((second[1], held[2], held[3]))[0]
    front = near(0) + far(0) + near(1) + far(1) + near(2) + near(3)
    done = late(front, third)
    second[2], second[3], done = lax.optimization_barrier((second[2], second[3], done))
    return done, front, far(2) + far(3), early, middle, third


def placed(n):
    mine = lax.axis_index("train").astype(jnp.int32)
    if n != 32:
        return jnp.stack([mine * 0, mine * 0, mine]), n
    return jnp.stack([mine // 8, mine % 8, mine]), 8


def plan(entries):
    return [(chunk, lows) for _, chunk, lows in entries], [array for array, _, _ in entries]


def split(value):
    high = value.astype(BF16)
    return high, (value - high.astype(F32)).astype(BF16)


def dot3(left, right):
    lh, ll = split(left)
    rh, rl = split(right)
    dot = functools.partial(jnp.dot, preferred_element_type=F32)
    return dot(lh, rh) + (dot(lh, rl) + dot(ll, rh))


def one_hot(index_row, count):
    steps = lax.broadcasted_iota(jnp.int32, (count, index_row.shape[1]), 0)
    return (index_row == steps).astype(F32)


def weighted(rows, picked):
    ranks, tokens = rows.shape
    return (rows[:, None, :] * picked[None, :, :]).reshape(ranks * picked.shape[0], tokens)


def squares(raw, items):
    each = jnp.sum(raw * raw, axis=1, keepdims=True)
    return jnp.sum(each.reshape(RANK, items, 1), axis=0)


def pairs_of(steps):
    pairs = {}
    for k, (chunk, lows) in enumerate(steps):
        for s, low in enumerate(lows):
            pairs.setdefault((chunk, low // 2), []).append((k, s, low))
    return pairs


def project(steps, size, place_ref, x_ref, g_ref, refs, held, grad, inp):
    hi, lo = place_ref[0], place_ref[1]
    part = refs[0].shape[1] // 2
    pairs = pairs_of(steps)
    for p, places in enumerate(pairs.values()):
        for k, s, low in places:
            held[p, 0, (lo ^ low) & 1] = refs[k][s, 0:part, :]
            held[p, 1, (lo ^ low) & 1] = refs[k][s, part : 2 * part, :]
    width = 2 * part
    for p, ((chunk, _), places) in enumerate(pairs.items()):
        device = (hi ^ chunk) * size + ((lo ^ places[0][2]) & -2)
        columns = pl.ds(pl.multiple_of(device * part, width), width)
        more = jnp.dot(g_ref[:, columns], held[p, 0].reshape(width, PW), preferred_element_type=F32)
        grad = more if grad is None else grad + more
        more = jnp.dot(x_ref[:, columns], held[p, 1].reshape(width, PW), preferred_element_type=F32)
        inp = more if inp is None else inp + more
    return grad, inp


def begin_kernel(steps, size, place_ref, x_ref, g_ref, *rest):
    refs, (sums_ref, held) = rest[: len(steps)], rest[len(steps) :]
    grad, inp = project(steps, size, place_ref, x_ref, g_ref, refs, held, None, None)
    sums_ref[0] = grad
    sums_ref[1] = inp


def eval_kernel(steps, size, begun, place_ref, x_ref, g_ref, hidden_ref, back_ref, index_ref, *rest):
    refs, rest = rest[: len(steps)], rest[len(steps) :]
    pack_ref, held = rest[begun:]
    grad, inp = (rest[0][0], rest[0][1]) if begun else (None, None)
    grad, inp = project(steps, size, place_ref, x_ref, g_ref, refs, held, grad, inp)
    picked = one_hot(index_ref[...], EVAL_ROLLOUTS)
    hidden, back = hidden_ref[...], back_ref[...]
    total = squares(dot3(weighted(hidden, picked), grad), EVAL_ROLLOUTS)
    total = total + squares(dot3(weighted(back, picked), inp), EVAL_ROLLOUTS)
    scale = lax.rsqrt(total * (1.0 / K) + EPS)
    per_token = jnp.sum(picked * scale, axis=0, keepdims=True)
    tokens = x_ref.shape[0]
    base = 2 * tokens
    pack_ref[0, 0:tokens, :] = grad.astype(BF16)
    pack_ref[0, tokens:base, :] = inp.astype(BF16)
    pack_ref[0, base : base + RANK, 0:tokens] = (hidden * per_token).astype(BF16)
    pack_ref[0, base : base + RANK, tokens:base] = (back * per_token).astype(BF16)
    index = jnp.broadcast_to(index_ref[...].astype(F32), (RANK, tokens)).astype(BF16)
    pack_ref[0, base + RANK : base + 2 * RANK, 0:tokens] = index
    pack_ref[0, base + RANK : base + 2 * RANK, tokens:base] = index


def train_kernel(steps, size, side, place_ref, act_ref, adapter_ref, *rest):
    refs, rest = rest[: len(steps)], rest[len(steps) :]
    hi, lo = place_ref[0], place_ref[1]
    part = refs[0].shape[1] // 2
    held = rest[-1]
    for ref, (chunk, lows) in zip(refs, steps):
        for s, low in enumerate(lows):
            held[(hi ^ chunk) * size + (lo ^ low)] = ref[s, side * part : (side + 1) * part, :]
    width = held.shape[0] * part
    factor = lax.dot_general(adapter_ref[...], act_ref[...], NT, preferred_element_type=F32)
    values = jnp.dot(act_ref[...], held[...].reshape(width, PW), preferred_element_type=F32)
    values_ref, factor_ref = rest[:2]
    values_ref[...] = values
    factor_ref[...] = factor


def feats_kernel(values_ref, back_ref, inputs_ref, hidden_ref, index_ref, feats_ref):
    picked = one_hot(index_ref[...], TRAIN_EXAMPLES)
    raw_a = dot3(weighted(hidden_ref[...], picked), values_ref[...])
    raw_b = dot3(weighted(back_ref[...], picked), inputs_ref[...])
    total = squares(raw_a, TRAIN_EXAMPLES) + squares(raw_b, TRAIN_EXAMPLES)
    scale = lax.rsqrt(total * (1.0 / K) + EPS)[None]
    shape = (RANK, TRAIN_EXAMPLES, PW)
    feats_ref[0] = (raw_a.reshape(shape) * scale).reshape(RANK * TRAIN_EXAMPLES, PW).astype(BF16)
    feats_ref[1] = (raw_b.reshape(shape) * scale).reshape(RANK * TRAIN_EXAMPLES, PW).astype(BF16)


def make_tiles(steps, size, place_ref, feats_ref, refs, tiles_ref):
    hi, lo = place_ref[0], place_ref[1]
    tokens = refs[0].shape[1] // 2 - RANK
    base = 2 * tokens
    shape = (RANK, TRAIN_EXAMPLES, base)
    dot = functools.partial(lax.dot_general, dimension_numbers=NT, preferred_element_type=F32)
    for ref, (chunk, lows) in zip(refs, steps):
        for s in range(0, len(lows), 2):
            two = slice(s, s + 2)
            grad = ref[two, 0:tokens, :].reshape(base, PW)
            inp = ref[two, tokens:base, :].reshape(base, PW)
            coef = ref[two, base : base + RANK, :].astype(F32)
            hidden = jnp.concatenate([coef[0, :, 0:tokens], coef[1, :, 0:tokens]], axis=1)
            back = jnp.concatenate([coef[0, :, tokens:], coef[1, :, tokens:]], axis=1)
            mixed = jnp.sum(dot(feats_ref[0], grad).reshape(shape) * hidden[:, None, :], axis=0)
            mixed = mixed + jnp.sum(dot(feats_ref[1], inp).reshape(shape) * back[:, None, :], axis=0)
            high, low = split(mixed)
            for k in range(2):
                index = ref[s + k, base + RANK : base + 2 * RANK, 0:tokens].astype(F32)
                picked = one_hot(index[0:1].astype(jnp.int32), EVAL_ROLLOUTS).astype(BF16)
                lanes = slice(k * tokens, (k + 1) * tokens)
                tile = dot(picked, high[:, lanes]) + dot(picked, low[:, lanes])
                tiles_ref[(hi ^ chunk) * size + (lo ^ lows[s + k])] = tile


def tile_kernel(steps, size, place_ref, feats_ref, *rest):
    make_tiles(steps, size, place_ref, feats_ref, rest[: len(steps)], rest[len(steps)])


def score_kernel(steps, earlier, size, place_ref, pairing_ref, live_ref, feats_ref, *rest):
    refs, rest = rest[: len(steps)], rest[len(steps) :]
    out_ref, tiles = rest[-2:]
    hi, lo, mine = place_ref[0], place_ref[1], place_ref[2]
    make_tiles(steps, size, place_ref, feats_ref, refs, tiles)
    for ref, known in zip(rest, earlier):
        for chunk, lows in known:
            for low in lows:
                device = (hi ^ chunk) * size + (lo ^ low)
                tiles[device] = ref[device]
    for slot in range(SLOTS):
        factor = jnp.where(slot < live_ref[mine], 1.0 / K**0.5, 0.0)
        out_ref[0, slot] = tiles[pairing_ref[slot, mine]] * factor


def call(kernel, out_shape, scratch, flops, name, scalars, *arrays):
    return pl.pallas_call(
        kernel,
        out_shape=out_shape,
        in_specs=[SMEM] * len(scalars) + [VMEM] * len(arrays),
        out_specs=jax.tree.map(lambda _: VMEM, out_shape),
        scratch_shapes=scratch,
        compiler_params=pltpu.CompilerParams(vmem_limit_bytes=28 * 1024 * 1024),
        cost_estimate=pl.CostEstimate(flops=flops // 1000, bytes_accessed=4096, transcendentals=0),
        name=name,
    )(*scalars, *arrays)


def per_device(
    n,
    train_layer_input,
    train_output_gradient,
    train_example_index,
    eval_layer_input,
    eval_output_gradient,
    eval_rollout_index,
    adapter_down,
    adapter_up,
    gradient_projector,
    input_projector,
    paired_eval_index,
    live_slot_count,
):
    place, size = placed(n)
    tokens = eval_layer_input.shape[0]
    part = gradient_projector.shape[0]
    acts = (eval_layer_input, eval_output_gradient)
    sums = jax.ShapeDtypeStruct((2, tokens, PW), F32)
    tiles_shape = (n, EVAL_ROLLOUTS, TRAIN_EXAMPLES)

    def down(x):
        return lax.dot_general(adapter_down, x, (((0,), (1,)), ((), ())), preferred_element_type=F32)

    def up(g):
        return lax.dot_general(adapter_up, g, NT, preferred_element_type=F32)

    def room(steps):
        return [pltpu.VMEM((len(pairs_of(steps)), 2, 2, part, PW), BF16)]

    def begin(front, early):
        steps, arrays = plan(front)
        place = early[2]
        kernel = functools.partial(begin_kernel, steps, size)
        return call(kernel, sums, room(steps), 8 * 10**8, "eval_begin", [place], *acts, *arrays)

    early = (down(eval_layer_input), up(eval_output_gradient), place)
    block = jnp.concatenate([gradient_projector, input_projector], axis=0)[None]
    begun, front, back, early, _, _ = gather_blocks(block, n, early, tuple, tuple, begin)
    place = early[2]
    steps, arrays = plan(back)
    extra = [] if begun is None else [begun]
    pack = call(
        functools.partial(eval_kernel, steps, size, len(extra)),
        jax.ShapeDtypeStruct((1, 2 * (tokens + RANK), PW), BF16),
        room(steps),
        10**9,
        "eval_factors",
        [place],
        *acts,
        early[0],
        early[1],
        eval_rollout_index,
        *arrays,
        *extra,
    )
    every, everything = plan(front + back)
    held = [pltpu.VMEM((n, part, PW), BF16)]
    rows = RANK * TRAIN_EXAMPLES
    values_shape = jax.ShapeDtypeStruct((train_layer_input.shape[0], PW), F32)
    factor_shape = jax.ShapeDtypeStruct((RANK, train_layer_input.shape[0]), F32)

    def train_side(side, place, acts, adapter):
        name = ("train_gradient_side", "train_input_side")[side]
        kernel = functools.partial(train_kernel, every, size, side)
        shapes = [values_shape, factor_shape]
        return call(kernel, shapes, held, 2 * 10**9, name, [place], acts, adapter, *everything)

    def gradient_side(early):
        return early[0], *train_side(0, early[0], train_output_gradient, adapter_up)

    def input_side(middle):
        return *middle[1:], *train_side(1, middle[0], train_layer_input, adapter_down.T)

    def features(sides):
        shape = jax.ShapeDtypeStruct((2, rows, PW), BF16)
        return call(feats_kernel, shape, [], 10**9, "train_features", [], *sides, train_example_index)

    def tile(front, feats):
        steps, arrays = plan(front)
        kernel = functools.partial(tile_kernel, steps, size)
        return call(kernel, jax.ShapeDtypeStruct(tiles_shape, F32), [], 10**9, "front_tiles", [place], feats, *arrays)

    def late(front, sides):
        feats = features(sides)
        return tile(front, feats), feats

    done, front, back, _, _, sides = gather_blocks(pack, n, (place,), gradient_side, input_side, late)
    extra, earlier = [], []
    if done is None:
        feats = features(sides)
    else:
        tiles, feats = done
        own, back = back[0::2], back[1::2]
        extra, earlier = [tiles, tile(own, feats)], [plan(front)[0], plan(own)[0]]
    steps, arrays = plan(back)
    scores = call(
        functools.partial(score_kernel, steps, earlier, size),
        jax.ShapeDtypeStruct((1, SLOTS, EVAL_ROLLOUTS, TRAIN_EXAMPLES), F32),
        [pltpu.VMEM(tiles_shape, F32)],
        10**9,
        "score_tiles",
        [place, paired_eval_index.T, live_slot_count],
        feats,
        *arrays,
        *extra,
    )
    return jnp.swapaxes(scores, 2, 3)


def solution(mesh):
    in_specs = (
        P(("parts", "train"), None),
        P(("parts", "train"), None),
        P(("parts", "train"), None),
        P(("parts", "train"), None),
        P(("parts", "train"), None),
        P(("parts", "train"), None),
        P(),
        P(),
        P("train", None),
        P("train", None),
        P("parts", None),
        P("parts"),
    )
    out_specs = P(("parts", "train"), None, None, None)
    return jax.shard_map(
        functools.partial(per_device, mesh.shape["train"]),
        mesh=mesh,
        in_specs=in_specs,
        out_specs=out_specs,
        check_vma=False,
    )
```
